128 devices in a mesh: tm: 4 (over x), state: 32 (over z, y, core).
Axes of the slice: x: 4, y: 4, z: 4, core: 2. Of those that a mesh axis runs over, the one named last changes fastest.
Arguments:
- transitions: bfloat16 [8, 1024, 1024], P('tm', 'state'), may hold values from -0.15 to 1.15
- gain: bfloat16 [1024, 128], P('state'), may hold values from -0.25 to 0.25
- obs_op: bfloat16 [128, 1024], P(None, 'state'), may hold values from -0.1875 to 0.1875
- observations: float32 [8, 128], P('tm'), may hold values from -6 to 6
- start: float32 [1024], P('state'), may hold values from -6 to 6
Outputs:
- means: float32 [8, 1024], P('tm', 'state')
- block_ends: float32 [4, 1024], P('tm', 'state')
The draws below stay inside these ranges and needn't reach their ends.
All inputs are finite; a program needn't handle non-finite values.
Results may differ from the reference program's by a relative error of at most 0.0047.
Values may be sent and summed in bfloat16 or wider, within the bound.
No kernel may reach another device: no remote copies, remote signals or barrier semaphores. Data moves between devices by JAX's collectives and lax.ppermute only.
A program may use at most 64 MiB of HBM per device.

```python
import math
import jax
import jax.numpy as jnp
from jax import lax

N = 1024
OBS = 128
STEPS_DEV = 2
BLOCKS = 4
TOTAL_STEPS = 8


def draw_transitions(key, part):
    key = jax.random.fold_in(key, 11)
    rate_key, shock_key, noise_key = jax.random.split(key, 3)
    rate = jnp.exp(jax.random.uniform(rate_key, (N,), jnp.float32, math.log(0.01), math.log(0.12)))
    retain_flags = 1.0 - rate
    shock_event = jnp.where(jax.random.bernoulli(shock_key, 4.0 / TOTAL_STEPS, (TOTAL_STEPS,)), 0.6, 1.0).astype(jnp.float32)
    noise = jax.random.normal(noise_key, (TOTAL_STEPS, N, N), jnp.float32)
    noise = jnp.clip(noise, -4.5, 4.5)
    identity_matrix = jnp.eye(N, dtype=jnp.float32)
    diagonal_entries = identity_matrix[None, :, :] * (shock_event[:, None, None] * retain_flags[None, :, None])
    return (noise * (0.25 / N ** 0.5) + diagonal_entries).astype(jnp.bfloat16)


def level_of(own_key, extent, cuts, low, high):
    def one(position, shards_of):
        draws = jax.random.uniform(jax.random.fold_in(jax.random.fold_in(own_key, 6), position), (shards_of,), jnp.float32, low / len(cuts), high / len(cuts))
        return jnp.repeat(jnp.exp(draws), extent[position] // shards_of).reshape((-1,) + (1,) * (len(extent) - position - 1))

    level = one(*cuts[0])
    for cut in cuts[1:]:
        level = level * one(*cut)
    return level


def scatter_about(stream_key, extent, deviation, limit, cuts=(), kind=jnp.bfloat16):
    drawn = jax.random.normal(stream_key, extent, jnp.float32) * deviation
    if len(cuts) > 0:
        drawn = level_of(stream_key, extent, cuts, -0.22, 0.18) * drawn
    return jnp.clip(drawn, min=-limit, max=limit).astype(kind)


def setup_inputs(seed: int = 0) -> dict:
    streams_of = jax.random.split(jax.random.key(seed), 6)
    return {
        "transitions": draw_transitions(jax.random.fold_in(streams_of[5], 71), 0),
        "gain": scatter_about(streams_of[1], (N, OBS), (0.2 * OBS ** -0.5), 0.25, ((0, 32),)),
        "obs_op": scatter_about(streams_of[2], (OBS, N), N ** -0.5, 0.1875, ((1, 32),)),
        "observations": scatter_about(streams_of[3], (TOTAL_STEPS, OBS), 1.0, 6.0, ((0, 4),), jnp.float32),
        "start": scatter_about(streams_of[4], (N,), 1.0, 6.0, ((0, 32),), jnp.float32),
    }


def reference(transitions, gain, obs_op, observations, start):
    f32 = jnp.float32
    high = lax.Precision.HIGHEST
    projected = jnp.einsum('oj,kjn->kon', obs_op.astype(f32), transitions.astype(f32)).astype(jnp.bfloat16)
    corrected = jnp.einsum('io,kon->kin', gain.astype(f32), projected.astype(f32))
    models = (transitions.astype(f32) - corrected).astype(jnp.bfloat16)
    sources = jnp.einsum('io,ko->ki', gain.astype(f32), observations, precision=high)
    per_block = models.reshape(BLOCKS, STEPS_DEV, N, N)
    per_source = sources.reshape(BLOCKS, STEPS_DEV, N)
    summary_mat = per_block[:, 0].astype(f32)
    summary_vec = per_source[:, 0]
    for inner in range(1, STEPS_DEV):
        current = per_block[:, inner].astype(f32)
        summary_vec = jnp.einsum('bij,bj->bi', current, summary_vec, precision=high) + per_source[:, inner]
        summary_mat = jnp.einsum('bij,bjk->bik', current, summary_mat, precision=high)
    span = 1
    while span < BLOCKS:
        mine = summary_mat[span:]
        new_vec = jnp.einsum('bij,bj->bi', mine, summary_vec[:-span], precision=high) + summary_vec[span:]
        new_mat = jnp.einsum('bij,bjk->bik', mine, summary_mat[:-span], precision=high)
        summary_mat = jnp.concatenate([summary_mat[:span], new_mat], axis=0)
        summary_vec = jnp.concatenate([summary_vec[:span], new_vec], axis=0)
        span = span * 2
    ends = jnp.einsum('bij,j->bi', summary_mat, start, precision=high) + summary_vec
    firsts = jnp.concatenate([start[None, :], ends[:-1]], axis=0)
    state_now = firsts
    results = []
    for inner in range(STEPS_DEV):
        state_now = jnp.einsum('bij,bj->bi', per_block[:, inner].astype(f32), state_now, precision=high) + per_source[:, inner]
        results.append(state_now)
    return jnp.stack(results, axis=1).reshape(TOTAL_STEPS, N), ends
```

```python
import jax
import jax.numpy as jnp
from jax import lax
from jax.experimental import pallas as pl
from jax.experimental.pallas import tpu as pltpu
from jax.sharding import PartitionSpec as P

F32 = jnp.float32
BF16 = jnp.bfloat16
RING = 4
BLOCKS = 4
MATMUL = (((1,), (0,)), ((), ()))
BY_ROWS = (((1,), (1,)), ((), ()))
BY_COLUMNS = (((0,), (0,)), ((), ()))


def dot(left, right, dims):
    return lax.dot_general(left, right, dims, preferred_element_type=F32)


def split(x):
    high = x.astype(BF16)
    rest = x - high.astype(F32)
    mid = rest.astype(BF16)
    low = (rest - mid.astype(F32)).astype(BF16)
    return high, mid, low


def stacked(x, rows):
    pieces = jnp.concatenate([piece.astype(F32) for piece in split(x)], axis=0)
    pad = jnp.zeros((rows - pieces.shape[0], x.shape[1]), F32)
    return jnp.concatenate([pieces, pad], axis=0).astype(BF16)


def step(model, x, source):
    parts = dot(stacked(x, 16), model, BY_ROWS)
    return parts[0:1] + parts[1:2] + parts[2:3] + source


def pack_kernel(trans_ref, gain_ref, obs_ref, start_ref, out_ref):
    rows, width = trans_ref.shape[1], trans_ref.shape[2]
    out_ref[:, 0:width] = trans_ref[0]
    out_ref[:, width : 2 * width] = trans_ref[1]
    out_ref[:, 2 * width : 2 * width + 128] = gain_ref[...]
    eye = (
        lax.broadcasted_iota(jnp.int32, (rows, rows), 0)
        == lax.broadcasted_iota(jnp.int32, (rows, rows), 1)
    ).astype(F32).astype(BF16)
    below = jnp.concatenate([obs_ref[...], stacked(start_ref[...], 128)], axis=0)
    out_ref[:, 2 * width + 128 :] = dot(eye, below, BY_ROWS).astype(BF16)


def pack(transitions, gain, obs_op, start):
    rows, width = transitions.shape[1], transitions.shape[2]
    return pl.pallas_call(
        pack_kernel,
        out_shape=jax.ShapeDtypeStruct((rows, 2 * width + 384), BF16),
        compiler_params=pltpu.CompilerParams(vmem_limit_bytes=4 << 20),
        name="pack",
    )(transitions, gain, obs_op, start[None, :])


def own_lanes(x, shift, rows):
    return pltpu.roll(x, shift, 1)[:, 0:rows]


def emit(shift, rows, u, v, end_ref, means_ref, last_ref):
    end_ref[...] = v
    mine = own_lanes(jnp.concatenate([u, v] + [u] * 6, axis=0), shift, rows)
    means_ref[...] = mine[0:2]
    last_ref[...] = mine[1:2]


def build_kernel(
    where_ref, obs_ref, *refs
):
    parts = refs[0:8]
    m0_ref, m1_ref, src_ref, end_ref, means_ref, last_ref = refs[8:14]
    gains, starts, seen = refs[14:17]
    width = m0_ref.shape[1]
    rows = means_ref.shape[1]
    g = 2 * width
    total = None
    for part in parts:
        term = dot(part[:, g + 128 : g + 256], part[:, 0:g], BY_COLUMNS)
        total = term if total is None else total + term
    seen[...] = total.astype(BF16)
    for index, part in enumerate(parts):
        gain = part[:, g : g + 128]
        for k, out in enumerate((m0_ref, m1_ref)):
            fix = dot(gain, seen[:, k * width : (k + 1) * width], MATMUL)
            model = (part[:, k * width : (k + 1) * width].astype(F32) - fix).astype(BF16)
            for j in range(RING):
                at = pl.multiple_of(where_ref[index * RING + j], rows)
                out[pl.ds(at, rows), :] = model[j * rows : (j + 1) * rows]
        for j in range(RING):
            at = pl.multiple_of(where_ref[index * RING + j], rows)
            gains[pl.ds(at, rows), :] = gain[j * rows : (j + 1) * rows]
            starts[pl.ds(at, rows), :] = part[j * rows : (j + 1) * rows, g + 256 : g + 384]
    first = dot(stacked(obs_ref[0:1, :], 16), gains[...], BY_ROWS)
    second = dot(stacked(obs_ref[1:2, :], 16), gains[...], BY_ROWS)
    s0 = first[0:1] + first[1:2] + first[2:3]
    s1 = second[0:1] + second[1:2] + second[2:3]
    src_ref[0:1, :] = s0
    src_ref[1:2, :] = s1
    pick = (
        lax.broadcasted_iota(jnp.int32, (16, 128), 0)
        == lax.broadcasted_iota(jnp.int32, (16, 128), 1)
    ).astype(F32).astype(BF16)
    begun = dot(pick, starts[...], BY_ROWS)
    x = begun[0:1] + begun[1:2] + begun[2:3]
    u = step(m0_ref[...], x, s0)
    v = step(m1_ref[...], u, s1)
    emit(where_ref[32], rows, u, v, end_ref, means_ref, last_ref)


def chain_shapes(rows, width):
    return (
        jax.ShapeDtypeStruct((1, width), F32),
        jax.ShapeDtypeStruct((2, rows), F32),
        jax.ShapeDtypeStruct((1, rows), F32),
    )


def build(where, observations, parts, rows, width):
    smem = pl.BlockSpec(memory_space=pltpu.SMEM)
    vmem = pl.BlockSpec(memory_space=pltpu.VMEM)
    return pl.pallas_call(
        build_kernel,
        in_specs=[smem] + [vmem] * 9,
        out_shape=(
            jax.ShapeDtypeStruct((width, width), BF16),
            jax.ShapeDtypeStruct((width, width), BF16),
            jax.ShapeDtypeStruct((2, width), F32),
        )
        + chain_shapes(rows, width),
        scratch_shapes=[
            pltpu.VMEM((width, 128), BF16),
            pltpu.VMEM((width, 128), BF16),
            pltpu.VMEM((128, 2 * width), BF16),
        ],
        compiler_params=pltpu.CompilerParams(vmem_limit_bytes=24 << 20),
        name="build",
    )(where, observations, *parts)


def advance_kernel(
    at_ref, m0_ref, m1_ref, src_ref, x_ref, end0, means0, last0, end_ref, means_ref, last_ref
):
    rows = means_ref.shape[1]

    @pl.when(at_ref[1] == 1)
    def _():
        u = step(m0_ref[...], x_ref[...], src_ref[0:1, :])
        v = step(m1_ref[...], u, src_ref[1:2, :])
        emit(at_ref[0], rows, u, v, end_ref, means_ref, last_ref)

    @pl.when(at_ref[1] == 0)
    def _():
        end_ref[...] = end0[...]
        means_ref[...] = means0[...]
        last_ref[...] = last0[...]


def advance(at, m0, m1, sources, x, before):
    smem = pl.BlockSpec(memory_space=pltpu.SMEM)
    vmem = pl.BlockSpec(memory_space=pltpu.VMEM)
    return pl.pallas_call(
        advance_kernel,
        in_specs=[smem] + [vmem] * 7,
        out_shape=chain_shapes(before[1].shape[1], m0.shape[1]),
        compiler_params=pltpu.CompilerParams(vmem_limit_bytes=8 << 20),
        name="advance",
    )(at, m0, m1, sources, x, *before)


def place(index):
    return index // (2 * RING), (index // 2) % RING, index % 2


def index_of(z, y, core):
    return ((z % RING) * RING + y % RING) * 2 + core


def along(first, distance):
    route = []
    for index in range(2 * RING * RING):
        z, y, core = place(index)
        if (core == 0) == first:
            route.append((index, index_of(z, y + distance, core)))
        else:
            route.append((index, index_of(z + distance, y, core)))
    return route


SWAP = [(index, index ^ 1) for index in range(2 * RING * RING)]


def shards(transitions, gain, obs_op, observations, start):
    here = lax.axis_index("tm")
    me = lax.axis_index("state")
    rows, width = transitions.shape[1], transitions.shape[2]
    z, y, core = place(me)

    offsets = []
    for side in (core, 1 - core):
        for far in range(RING):
            for near in range(RING):
                zz = jnp.where(side == 0, z - far, z - near)
                yy = jnp.where(side == 0, y - near, y - far)
                offsets.append(rows * index_of(zz, yy, side))
    shift = (width - rows * me) % width
    where = jnp.stack(offsets + [shift]).astype(jnp.int32)

    mine = pack(transitions, gain, obs_op, start)
    near = [mine] + [lax.ppermute(mine, "state", along(True, d)) for d in range(1, RING)]
    line = jnp.concatenate(near, axis=0)
    own = [line] + [lax.ppermute(line, "state", along(False, d)) for d in range(1, RING)]
    others = [lax.ppermute(part, "state", SWAP) for part in own]

    m0, m1, sources, *state = build(where, observations, own + others, rows, width)
    for block in range(1, BLOCKS):
        x = lax.ppermute(state[0], "tm", [(block - 1, block)])
        at = jnp.stack([shift, (here == block).astype(jnp.int32)]).astype(jnp.int32)
        state = advance(at, m0, m1, sources, x, state)
    return state[1], state[2]


def solution(mesh):
    in_specs = (
        P("tm", "state", None),
        P("state", None),
        P(None, "state"),
        P("tm", None),
        P("state"),
    )
    out_specs = (P("tm", "state"), P("tm", "state"))
    return jax.shard_map(shards, mesh=mesh, in_specs=in_specs, out_specs=out_specs, check_vma=False)
```

```python
import functools

import jax
import jax.numpy as jnp
from jax import lax
from jax.experimental import pallas as pl
from jax.experimental.pallas import tpu as pltpu
from jax.sharding import PartitionSpec as P

F32 = jnp.float32
BF16 = jnp.bfloat16
RING = 4
BLOCKS = 4
MATMUL = (((1,), (0,)), ((), ()))
BY_ROWS = (((1,), (1,)), ((), ()))
BY_COLUMNS = (((0,), (0,)), ((), ()))


def dot(left, right, dims):
    return lax.dot_general(left, right, dims, preferred_element_type=F32)


def split(x):
    high = x.astype(BF16)
    rest = x - high.astype(F32)
    mid = rest.astype(BF16)
    low = (rest - mid.astype(F32)).astype(BF16)
    return high, mid, low


def stacked(x, rows):
    pieces = jnp.concatenate([piece.astype(F32) for piece in split(x)], axis=0)
    pad = jnp.zeros((rows - pieces.shape[0], x.shape[1]), F32)
    return jnp.concatenate([pieces, pad], axis=0).astype(BF16)


def step(model, x, source):
    parts = dot(stacked(x, 16), model, BY_ROWS)
    return parts[0:1] + parts[1:2] + parts[2:3] + source


def pack_kernel(trans_ref, gain_ref, obs_ref, start_ref, out_ref, held, sems):
    rows, width = trans_ref.shape[1], trans_ref.shape[2]
    g = 2 * width
    copies = [
        pltpu.make_async_copy(start_ref, held, sems.at[0]),
        pltpu.make_async_copy(trans_ref.at[0], out_ref.at[:, 0:width], sems.at[1]),
        pltpu.make_async_copy(trans_ref.at[1], out_ref.at[:, width:g], sems.at[2]),
        pltpu.make_async_copy(obs_ref, out_ref.at[:, g : g + 128], sems.at[3]),
        pltpu.make_async_copy(gain_ref, out_ref.at[:, g + 128 : g + 256], sems.at[4]),
    ]
    for copy in copies:
        copy.start()
    eye = (
        lax.broadcasted_iota(jnp.int32, (rows, rows), 0)
        == lax.broadcasted_iota(jnp.int32, (rows, rows), 1)
    ).astype(F32).astype(BF16)
    copies[0].wait()
    out_ref[:, g + 256 :] = dot(eye, stacked(held[...], 128), BY_ROWS).astype(BF16)
    for copy in copies[1:]:
        copy.wait()


def pack(transitions, gain, obs_op, start):
    rows, width = transitions.shape[1], transitions.shape[2]
    return pl.pallas_call(
        pack_kernel,
        in_specs=[pl.BlockSpec(memory_space=pltpu.HBM)] * 4,
        out_shape=jax.ShapeDtypeStruct((rows, 2 * width + 384), BF16),
        scratch_shapes=[pltpu.VMEM((1, rows), F32), pltpu.SemaphoreType.DMA((5,))],
        compiler_params=pltpu.CompilerParams(vmem_limit_bytes=4 << 20),
        name="pack",
    )(*(pltpu.with_memory_space_constraint(x, pltpu.HBM) for x in (transitions, gain, obs_op.T, start[None, :])))


def own_lanes(x, shift, rows):
    return pltpu.roll(x, shift, 1)[:, 0:rows]


def emit(shift, rows, u, v, end_ref, means_ref, last_ref):
    end_ref[...] = v
    mine = own_lanes(jnp.concatenate([u, v] + [u] * 6, axis=0), shift, rows)
    means_ref[...] = mine[0:2]
    last_ref[...] = mine[1:2]


def place(index):
    return index // (2 * RING), (index // 2) % RING, index % 2


def index_of(z, y, core):
    return ((z % RING) * RING + y % RING) * 2 + core


EARLY, LATE = (0, 1, RING - 1), (2,)


def row_offsets(rows, fars):
    z, y, core = place(lax.axis_index("state"))
    z, y = z + RING, y + RING
    offsets = []
    for side in (core, 1 - core):
        for far in fars:
            for near in range(RING):
                dz = far + side * (near - far)
                dy = near + side * (far - near)
                offsets.append(rows * index_of(z - dz, y - dy, side))
    return offsets


def put_rows(parts, fars, out_ref):
    rows = parts[0].shape[0] // RING
    where = row_offsets(rows, fars)
    for index, part in enumerate(parts):
        for j in range(RING):
            at = pl.multiple_of(where[index * RING + j], rows)
            out_ref[pl.ds(at, rows), :] = part[j * rows : (j + 1) * rows, :]


def lanes_shift(rows, width):
    return lax.rem(width - rows * lax.axis_index("state"), width)


def early_kernel(*refs):
    put_rows(refs[:-1], EARLY, refs[-1])


def early(parts, width):
    vmem = pl.BlockSpec(memory_space=pltpu.VMEM)
    return pl.pallas_call(
        early_kernel,
        in_specs=[vmem] * len(parts),
        out_shape=jax.ShapeDtypeStruct((width, parts[0].shape[1]), BF16),
        compiler_params=pltpu.CompilerParams(vmem_limit_bytes=4 << 20),
        name="early",
    )(*parts)


def total(parts):
    return parts[0:1] + parts[1:2] + parts[2:3]


def late_kernel(obs_ref, part0, part1, held_ref, all_ref, src_ref, end_ref, means_ref, last_ref, seen):
    del held_ref
    width = all_ref.shape[0]
    rows = means_ref.shape[1]
    g = 2 * width
    put_rows((part0, part1), LATE, all_ref)
    is_first = lax.axis_index("tm") == 0

    @pl.when(is_first)
    def _():
        pick = (
            lax.broadcasted_iota(jnp.int32, (16, 128), 0)
            == lax.broadcasted_iota(jnp.int32, (16, 128), 1)
        ).astype(F32).astype(BF16)
        x = total(dot(pick, all_ref[:, g + 256 : g + 384], BY_ROWS))
        states = []
        for k in range(2):
            y = total(dot(stacked(x, 16), all_ref[:, k * width : (k + 1) * width], BY_ROWS))
            seen_y = total(dot(stacked(y, 16), all_ref[:, g : g + 128], MATMUL))
            missed = stacked(obs_ref[k : k + 1, :] - seen_y, 16)
            x = y + total(dot(missed, all_ref[:, g + 128 : g + 256], BY_ROWS))
            states.append(x)
        src_ref[...] = jnp.zeros_like(src_ref)
        emit(lanes_shift(rows, width), rows, *states, end_ref, means_ref, last_ref)

    @pl.when(jnp.logical_not(is_first))
    def _():
        for k in range(2):
            source = dot(stacked(obs_ref[k : k + 1, :], 16), all_ref[:, g + 128 : g + 256], BY_ROWS)
            src_ref[k : k + 1, :] = total(source)
        seen[...] = dot(all_ref[:, g : g + 128], all_ref[:, 0:g], BY_COLUMNS).astype(BF16)
        for at in range(0, width, 128):
            fix = dot(all_ref[at : at + 128, g + 128 : g + 256], seen[...], MATMUL)
            model = all_ref[at : at + 128, 0:g].astype(F32) - fix
            all_ref[at : at + 128, 0:g] = model.astype(BF16)
        end_ref[...] = jnp.zeros_like(end_ref)
        means_ref[...] = jnp.zeros_like(means_ref)
        last_ref[...] = jnp.zeros_like(last_ref)


def chain_shapes(rows, width):
    return (
        jax.ShapeDtypeStruct((1, width), F32),
        jax.ShapeDtypeStruct((2, rows), F32),
        jax.ShapeDtypeStruct((1, rows), F32),
    )


def late(observations, parts, held, rows):
    vmem = pl.BlockSpec(memory_space=pltpu.VMEM)
    width, lanes = held.shape
    return pl.pallas_call(
        late_kernel,
        in_specs=[vmem] * 4,
        out_shape=(
            jax.ShapeDtypeStruct((width, lanes), BF16),
            jax.ShapeDtypeStruct((2, width), F32),
        )
        + chain_shapes(rows, width),
        scratch_shapes=[pltpu.VMEM((128, 2 * width), BF16)],
        input_output_aliases={3: 0},
        compiler_params=pltpu.CompilerParams(vmem_limit_bytes=16 << 20),
        name="late",
    )(observations, *parts, held)


def advance_kernel(
    block, all_ref, src_ref, x_ref, end0, means0, last0, end_ref, means_ref, last_ref
):
    rows, width = means_ref.shape[1], all_ref.shape[0]
    mine = lax.axis_index("tm") == block

    @pl.when(mine)
    def _():
        u = step(all_ref[:, 0:width], x_ref[...], src_ref[0:1, :])
        v = step(all_ref[:, width : 2 * width], u, src_ref[1:2, :])
        emit(lanes_shift(rows, width), rows, u, v, end_ref, means_ref, last_ref)

    @pl.when(jnp.logical_not(mine))
    def _():
        end_ref[...] = end0[...]
        means_ref[...] = means0[...]
        last_ref[...] = last0[...]


def advance(block, held, sources, x, before):
    vmem = pl.BlockSpec(memory_space=pltpu.VMEM)
    return pl.pallas_call(
        functools.partial(advance_kernel, block),
        in_specs=[vmem] * 6,
        out_shape=chain_shapes(before[1].shape[1], held.shape[0]),
        compiler_params=pltpu.CompilerParams(vmem_limit_bytes=8 << 20),
        name="advance",
    )(held, sources, x, *before)


def along(first, distance):
    route = []
    for index in range(2 * RING * RING):
        z, y, core = place(index)
        if (core == 0) == first:
            route.append((index, index_of(z, y + distance, core)))
        else:
            route.append((index, index_of(z + distance, y, core)))
    return route


SWAP = [(index, index ^ 1) for index in range(2 * RING * RING)]


def shards(transitions, gain, obs_op, observations, start):
    rows, width = transitions.shape[1], transitions.shape[2]
    mine = pack(transitions, gain, obs_op, start)
    near = [mine] + [lax.ppermute(mine, "state", along(True, d)) for d in range(1, RING)]
    line = jnp.concatenate(near, axis=0)
    ahead = lax.ppermute(line, "state", along(False, 1))
    behind = lax.ppermute(line, "state", along(False, RING - 1))
    half = line.shape[0] // 2
    across = [
        lax.ppermute(ahead[:half], "state", along(False, 1)),
        lax.ppermute(behind[half:], "state", along(False, RING - 1)),
    ]
    across = jnp.concatenate(across, axis=0)
    near_parts = [line, ahead, behind]
    near_parts += [lax.ppermute(part, "state", SWAP) for part in near_parts]
    held = early(near_parts, width)
    held, sources, *state = late(
        observations, (across, lax.ppermute(across, "state", SWAP)), held, rows
    )
    for block in range(1, BLOCKS):
        x = lax.ppermute(state[0], "tm", [(block - 1, block)])
        state = advance(block, held, sources, x, state)
    return state[1], state[2]


def solution(mesh):
    in_specs = (
        P("tm", "state", None),
        P("state", None),
        P(None, "state"),
        P("tm", None),
        P("state"),
    )
    out_specs = (P("tm", "state"), P("tm", "state"))
    return jax.shard_map(shards, mesh=mesh, in_specs=in_specs, out_specs=out_specs, check_vma=False)
```

```python
import functools

import jax
import jax.numpy as jnp
from jax import lax
from jax.experimental import pallas as pl
from jax.experimental.pallas import tpu as pltpu
from jax.sharding import PartitionSpec as P

F32 = jnp.float32
BF16 = jnp.bfloat16
RING = 4
BLOCKS = 4
MATMUL = (((1,), (0,)), ((), ()))
BY_ROWS = (((1,), (1,)), ((), ()))
BY_COLUMNS = (((0,), (0,)), ((), ()))


def dot(left, right, dims):
    return lax.dot_general(left, right, dims, preferred_element_type=F32)


def split(x):
    high = x.astype(BF16)
    rest = x - high.astype(F32)
    mid = rest.astype(BF16)
    low = (rest - mid.astype(F32)).astype(BF16)
    return high, mid, low


def stacked(x, rows):
    pieces = jnp.concatenate([piece.astype(F32) for piece in split(x)], axis=0)
    pad = jnp.zeros((rows - pieces.shape[0], x.shape[1]), F32)
    return jnp.concatenate([pieces, pad], axis=0).astype(BF16)


def step(model, x, source):
    parts = dot(stacked(x, 16), model, BY_ROWS)
    return parts[0:1] + parts[1:2] + parts[2:3] + source


def pack_kernel(trans_ref, gain_ref, obs_ref, start_ref, out_ref, held, sems):
    rows, width = trans_ref.shape[1], trans_ref.shape[2]
    g = 2 * width
    copies = [
        pltpu.make_async_copy(start_ref, held, sems.at[0]),
        pltpu.make_async_copy(trans_ref.at[0], out_ref.at[:, 0:width], sems.at[1]),
        pltpu.make_async_copy(trans_ref.at[1], out_ref.at[:, width:g], sems.at[2]),
        pltpu.make_async_copy(obs_ref, out_ref.at[:, g : g + 128], sems.at[3]),
        pltpu.make_async_copy(gain_ref, out_ref.at[:, g + 128 : g + 256], sems.at[4]),
    ]
    for copy in copies:
        copy.start()
    eye = (
        lax.broadcasted_iota(jnp.int32, (rows, rows), 0)
        == lax.broadcasted_iota(jnp.int32, (rows, rows), 1)
    ).astype(F32).astype(BF16)
    copies[0].wait()
    out_ref[:, g + 256 :] = dot(eye, stacked(held[...], 128), BY_ROWS).astype(BF16)
    for copy in copies[1:]:
        copy.wait()


def pack(transitions, gain, obs_op, start):
    rows, width = transitions.shape[1], transitions.shape[2]
    return pl.pallas_call(
        pack_kernel,
        in_specs=[pl.BlockSpec(memory_space=pltpu.HBM)] * 4,
        out_shape=jax.ShapeDtypeStruct((rows, 2 * width + 384), BF16),
        scratch_shapes=[pltpu.VMEM((1, rows), F32), pltpu.SemaphoreType.DMA((5,))],
        compiler_params=pltpu.CompilerParams(vmem_limit_bytes=4 << 20),
        name="pack",
    )(*(pltpu.with_memory_space_constraint(x, pltpu.HBM) for x in (transitions, gain, obs_op.T, start[None, :])))


def place(index):
    return index // (2 * RING), (index // 2) % RING, index % 2


def index_of(z, y, core):
    return ((z % RING) * RING + y % RING) * 2 + core


EARLY, LATE = (0, 1, RING - 1), (2,)


def row_offsets(rows, fars):
    z, y, core = place(lax.axis_index("state"))
    z, y = z + RING, y + RING
    offsets = []
    for side in (core, 1 - core):
        for far in fars:
            for near in range(RING):
                dz = far + side * (near - far)
                dy = near + side * (far - near)
                offsets.append(rows * index_of(z - dz, y - dy, side))
    return offsets


def put_rows(parts, fars, out_ref):
    rows = parts[0].shape[0] // RING
    where = row_offsets(rows, fars)
    for index, part in enumerate(parts):
        for j in range(RING):
            at = pl.multiple_of(where[index * RING + j], rows)
            out_ref[pl.ds(at, rows), :] = part[j * rows : (j + 1) * rows, :]


def lanes_shift(rows, width):
    return lax.rem(width - rows * lax.axis_index("state"), width)


def early_kernel(*refs):
    put_rows(refs[:-1], EARLY, refs[-1])


def early(parts, width):
    vmem = pl.BlockSpec(memory_space=pltpu.VMEM)
    return pl.pallas_call(
        early_kernel,
        in_specs=[vmem] * len(parts),
        out_shape=jax.ShapeDtypeStruct((width, parts[0].shape[1]), BF16),
        compiler_params=pltpu.CompilerParams(vmem_limit_bytes=4 << 20),
        name="early",
    )(*parts)


def total(parts):
    return parts[0:1] + parts[1:2] + parts[2:3]


def late_kernel(
    obs_ref, part0, part1, held_ref, all_ref, end_ref, kept_ref
):
    del held_ref
    width = all_ref.shape[0]
    g = 2 * width
    put_rows((part0, part1), LATE, all_ref)
    is_first = lax.axis_index("tm") == 0

    @pl.when(is_first)
    def _():
        pick = (
            lax.broadcasted_iota(jnp.int32, (16, 128), 0)
            == lax.broadcasted_iota(jnp.int32, (16, 128), 1)
        ).astype(F32).astype(BF16)
        x = total(dot(pick, all_ref[:, g + 256 : g + 384], BY_ROWS))
        states = []
        for k in range(2):
            y = total(dot(stacked(x, 16), all_ref[:, k * width : (k + 1) * width], BY_ROWS))
            seen_y = total(dot(stacked(y, 16), all_ref[:, g : g + 128], MATMUL))
            missed = stacked(obs_ref[k : k + 1, :] - seen_y, 16)
            x = y + total(dot(missed, all_ref[:, g + 128 : g + 256], BY_ROWS))
            states.append(x)
        kept_ref[...] = states[0]
        end_ref[...] = states[1]

    @pl.when(jnp.logical_not(is_first))
    def _():
        kept_ref[...] = jnp.zeros_like(kept_ref)
        end_ref[...] = jnp.zeros_like(end_ref)


def late(observations, parts, held):
    vmem = pl.BlockSpec(memory_space=pltpu.VMEM)
    width, lanes = held.shape
    row = jax.ShapeDtypeStruct((1, width), F32)
    return pl.pallas_call(
        late_kernel,
        in_specs=[vmem] * 4,
        out_shape=(jax.ShapeDtypeStruct((width, lanes), BF16), row, row),
        input_output_aliases={3: 0},
        compiler_params=pltpu.CompilerParams(vmem_limit_bytes=4 << 20),
        name="late",
    )(observations, *parts, held)


def models_kernel(obs_ref, held_ref, all_ref, both_ref, src_ref, seen):
    del held_ref
    width = all_ref.shape[0]
    g = 2 * width

    @pl.when(lax.axis_index("tm") > 0)
    def _():
        seen[...] = dot(all_ref[:, g : g + 128], all_ref[:, 0:g], BY_COLUMNS).astype(BF16)
        for at in range(0, width, 128):
            fix = dot(all_ref[at : at + 128, g + 128 : g + 256], seen[...], MATMUL)
            model = all_ref[at : at + 128, 0:g].astype(F32) - fix
            all_ref[at : at + 128, 0:g] = model.astype(BF16)
        sources = [
            total(dot(stacked(obs_ref[k : k + 1, :], 16), all_ref[:, g + 128 : g + 256], BY_ROWS))
            for k in range(2)
        ]
        src_ref[0:1, :] = sources[0]
        src_ref[1:2, :] = step(all_ref[:, width:g], sources[0], sources[1])
        for at in range(0, width, 256):
            rows = all_ref[at : at + 256, width:g]
            both_ref[at : at + 256, :] = dot(rows, all_ref[:, 0:width], MATMUL).astype(BF16)


def models(observations, held):
    vmem = pl.BlockSpec(memory_space=pltpu.VMEM)
    width, lanes = held.shape
    return pl.pallas_call(
        models_kernel,
        in_specs=[vmem] * 2,
        out_shape=(
            jax.ShapeDtypeStruct((width, lanes), BF16),
            jax.ShapeDtypeStruct((width, width), BF16),
            jax.ShapeDtypeStruct((2, width), F32),
        ),
        scratch_shapes=[pltpu.VMEM((128, 2 * width), BF16)],
        input_output_aliases={1: 0},
        compiler_params=pltpu.CompilerParams(vmem_limit_bytes=16 << 20),
        cost_estimate=pl.CostEstimate(
            flops=2 * width**3, bytes_accessed=8 * width * width, transcendentals=0
        ),
        name="models",
    )(observations, held)


def advance_kernel(block, both_ref, src_ref, x_ref, end0, kept0, end_ref, kept_ref):
    mine = lax.axis_index("tm") == block

    @pl.when(mine)
    def _():
        x = x_ref[...]
        end_ref[...] = step(both_ref[...], x, src_ref[1:2, :])
        kept_ref[...] = x

    @pl.when(jnp.logical_not(mine))
    def _():
        end_ref[...] = end0[...]
        kept_ref[...] = kept0[...]


def advance(block, both, sources, x, end, kept):
    row = jax.ShapeDtypeStruct(x.shape, F32)
    return pl.pallas_call(
        functools.partial(advance_kernel, block),
        in_specs=[pl.BlockSpec(memory_space=pltpu.VMEM)] * 5,
        out_shape=(row, row),
        compiler_params=pltpu.CompilerParams(vmem_limit_bytes=4 << 20),
        name="advance",
    )(both, sources, x, end, kept)


def finish_kernel(all_ref, both_ref, src_ref, x_ref, end_ref, kept_ref, means_ref, last_ref, held):
    rows, width = means_ref.shape[1], all_ref.shape[0]
    here = lax.axis_index("tm")
    held[0:1, :] = kept_ref[...]
    held[1:2, :] = end_ref[...]

    @pl.when(here == BLOCKS - 1)
    def _():
        held[0:1, :] = step(all_ref[:, 0:width], x_ref[...], src_ref[0:1, :])
        held[1:2, :] = step(both_ref[...], x_ref[...], src_ref[1:2, :])

    @pl.when(jnp.logical_and(here > 0, here < BLOCKS - 1))
    def _():
        held[0:1, :] = step(all_ref[:, 0:width], kept_ref[...], src_ref[0:1, :])

    mine = pltpu.roll(held[...], lanes_shift(rows, width), 1)
    means_ref[...] = mine[0:2, 0:rows]
    last_ref[...] = mine[1:2, 0:rows]


def finish(held, both, sources, x, end, kept, rows):
    return pl.pallas_call(
        finish_kernel,
        in_specs=[pl.BlockSpec(memory_space=pltpu.VMEM)] * 6,
        out_shape=(
            jax.ShapeDtypeStruct((2, rows), F32),
            jax.ShapeDtypeStruct((1, rows), F32),
        ),
        scratch_shapes=[pltpu.VMEM((8, held.shape[0]), F32)],
        compiler_params=pltpu.CompilerParams(vmem_limit_bytes=4 << 20),
        name="finish",
    )(held, both, sources, x, end, kept)


def along(first, distance):
    route = []
    for index in range(2 * RING * RING):
        z, y, core = place(index)
        if (core == 0) == first:
            route.append((index, index_of(z, y + distance, core)))
        else:
            route.append((index, index_of(z + distance, y, core)))
    return route


SWAP = [(index, index ^ 1) for index in range(2 * RING * RING)]


def shards(transitions, gain, obs_op, observations, start):
    rows, width = transitions.shape[1], transitions.shape[2]
    mine = pack(transitions, gain, obs_op, start)
    near = [mine] + [lax.ppermute(mine, "state", along(True, d)) for d in range(1, RING)]
    line = jnp.concatenate(near, axis=0)
    ahead = lax.ppermute(line, "state", along(False, 1))
    behind = lax.ppermute(line, "state", along(False, RING - 1))
    half = line.shape[0] // 2
    across = [
        lax.ppermute(ahead[:half], "state", along(False, 1)),
        lax.ppermute(behind[half:], "state", along(False, RING - 1)),
    ]
    across = jnp.concatenate(across, axis=0)
    near_parts = [line, ahead, behind]
    near_parts += [lax.ppermute(part, "state", SWAP) for part in near_parts]
    held = early(near_parts, width)
    across = (across, lax.ppermute(across, "state", SWAP))
    held, end, kept = late(observations, across, held)
    x = lax.ppermute(end, "tm", [(0, 1)])
    held, both, sources = models(observations, held)
    end, kept = advance(1, both, sources, x, end, kept)
    for block in range(2, BLOCKS - 1):
        x = lax.ppermute(end, "tm", [(block - 1, block)])
        end, kept = advance(block, both, sources, x, end, kept)
    x = lax.ppermute(end, "tm", [(BLOCKS - 2, BLOCKS - 1)])
    return finish(held, both, sources, x, end, kept, rows)


def solution(mesh):
    in_specs = (
        P("tm", "state", None),
        P("state", None),
        P(None, "state"),
        P("tm", None),
        P("state"),
    )
    out_specs = (P("tm", "state"), P("tm", "state"))
    return jax.shard_map(shards, mesh=mesh, in_specs=in_specs, out_specs=out_specs, check_vma=False)
```

```python
import functools

import jax
import jax.numpy as jnp
from jax import lax
from jax.experimental import pallas as pl
from jax.experimental.pallas import tpu as pltpu
from jax.sharding import PartitionSpec as P

F32 = jnp.float32
BF16 = jnp.bfloat16
RING = 4
BLOCKS = 4
MATMUL = (((1,), (0,)), ((), ()))
BY_ROWS = (((1,), (1,)), ((), ()))
BY_COLUMNS = (((0,), (0,)), ((), ()))


def dot(left, right, dims):
    return lax.dot_general(left, right, dims, preferred_element_type=F32)


def split(x):
    high = x.astype(BF16)
    rest = x - high.astype(F32)
    mid = rest.astype(BF16)
    low = (rest - mid.astype(F32)).astype(BF16)
    return high, mid, low


def stacked(x, rows):
    pieces = jnp.concatenate([piece.astype(F32) for piece in split(x)], axis=0)
    pad = jnp.zeros((rows - pieces.shape[0], x.shape[1]), F32)
    return jnp.concatenate([pieces, pad], axis=0).astype(BF16)


def step(model, x, source):
    parts = dot(stacked(x, 16), model, BY_ROWS)
    return parts[0:1] + parts[1:2] + parts[2:3] + source


def pack_kernel(trans_ref, gain_ref, obs_ref, start_ref, out_ref, held, sems):
    rows, width = trans_ref.shape[1], trans_ref.shape[2]
    g = 2 * width
    copies = [
        pltpu.make_async_copy(start_ref, held, sems.at[0]),
        pltpu.make_async_copy(trans_ref.at[0], out_ref.at[:, 0:width], sems.at[1]),
        pltpu.make_async_copy(trans_ref.at[1], out_ref.at[:, width:g], sems.at[2]),
        pltpu.make_async_copy(obs_ref, out_ref.at[:, g : g + 128], sems.at[3]),
        pltpu.make_async_copy(gain_ref, out_ref.at[:, g + 128 : g + 256], sems.at[4]),
    ]
    for copy in copies:
        copy.start()
    eye = (
        lax.broadcasted_iota(jnp.int32, (rows, rows), 0)
        == lax.broadcasted_iota(jnp.int32, (rows, rows), 1)
    ).astype(F32).astype(BF16)
    copies[0].wait()
    out_ref[:, g + 256 :] = dot(eye, stacked(held[...], 128), BY_ROWS).astype(BF16)
    for copy in copies[1:]:
        copy.wait()


def pack(transitions, gain, obs_op, start):
    rows, width = transitions.shape[1], transitions.shape[2]
    return pl.pallas_call(
        pack_kernel,
        in_specs=[pl.BlockSpec(memory_space=pltpu.HBM)] * 4,
        out_shape=jax.ShapeDtypeStruct((rows, 2 * width + 384), BF16),
        scratch_shapes=[pltpu.VMEM((1, rows), F32), pltpu.SemaphoreType.DMA((5,))],
        compiler_params=pltpu.CompilerParams(vmem_limit_bytes=4 << 20),
        name="pack",
    )(*(pltpu.with_memory_space_constraint(x, pltpu.HBM) for x in (transitions, gain, obs_op.T, start[None, :])))


def place(index):
    return index // (2 * RING), (index // 2) % RING, index % 2


def index_of(z, y, core):
    return ((z % RING) * RING + y % RING) * 2 + core


NEAR = (0, 3, 2, 1)
EARLY, LATE = (0, 1, RING - 1), (2,)


def row_offsets(rows, fars):
    z, y, core = place(lax.axis_index("state"))
    z, y = z + RING, y + RING
    offsets = []
    for side in (core, 1 - core):
        for far in fars:
            for near in NEAR:
                dz = far + side * (near - far)
                dy = near + side * (far - near)
                offsets.append(rows * index_of(z - dz, y - dy, side))
    return offsets


def put_rows(parts, fars, out_ref):
    rows = parts[0].shape[0] // RING
    where = row_offsets(rows, fars)
    for index, part in enumerate(parts):
        for j in range(RING):
            at = pl.multiple_of(where[index * RING + j], rows)
            out_ref[pl.ds(at, rows), :] = part[j * rows : (j + 1) * rows, :]


def lanes_shift(rows, width):
    return lax.rem(width - rows * lax.axis_index("state"), width)


def early_kernel(*refs):
    put_rows(refs[:-1], EARLY, refs[-1])


def early(parts, width):
    vmem = pl.BlockSpec(memory_space=pltpu.VMEM)
    return pl.pallas_call(
        early_kernel,
        in_specs=[vmem] * len(parts),
        out_shape=jax.ShapeDtypeStruct((width, parts[0].shape[1]), BF16),
        compiler_params=pltpu.CompilerParams(vmem_limit_bytes=4 << 20),
        name="early",
    )(*parts)


def total(parts):
    return parts[0:1] + parts[1:2] + parts[2:3]


def late_kernel(
    obs_ref, part0, part1, held_ref, all_ref, end_ref, kept_ref
):
    del held_ref
    width = all_ref.shape[0]
    g = 2 * width
    put_rows((part0, part1), LATE, all_ref)
    is_first = lax.axis_index("tm") == 0

    @pl.when(is_first)
    def _():
        pick = (
            lax.broadcasted_iota(jnp.int32, (16, 128), 0)
            == lax.broadcasted_iota(jnp.int32, (16, 128), 1)
        ).astype(F32).astype(BF16)
        x = total(dot(pick, all_ref[:, g + 256 : g + 384], BY_ROWS))
        states = []
        for k in range(2):
            y = total(dot(stacked(x, 16), all_ref[:, k * width : (k + 1) * width], BY_ROWS))
            seen_y = total(dot(stacked(y, 16), all_ref[:, g : g + 128], MATMUL))
            missed = stacked(obs_ref[k : k + 1, :] - seen_y, 16)
            x = y + total(dot(missed, all_ref[:, g + 128 : g + 256], BY_ROWS))
            states.append(x)
        kept_ref[...] = states[0]
        end_ref[...] = states[1]

    @pl.when(jnp.logical_not(is_first))
    def _():
        kept_ref[...] = jnp.zeros_like(kept_ref)
        end_ref[...] = jnp.zeros_like(end_ref)


def late(observations, parts, held):
    vmem = pl.BlockSpec(memory_space=pltpu.VMEM)
    width, lanes = held.shape
    row = jax.ShapeDtypeStruct((1, width), F32)
    return pl.pallas_call(
        late_kernel,
        in_specs=[vmem] * 4,
        out_shape=(jax.ShapeDtypeStruct((width, lanes), BF16), row, row),
        input_output_aliases={3: 0},
        compiler_params=pltpu.CompilerParams(vmem_limit_bytes=4 << 20),
        name="late",
    )(observations, *parts, held)


def models_kernel(obs_ref, held_ref, all_ref, src_ref, seen):
    del held_ref
    width = all_ref.shape[0]
    g = 2 * width

    @pl.when(lax.axis_index("tm") > 0)
    def _():
        seen[...] = dot(all_ref[:, g : g + 128], all_ref[:, 0:g], BY_COLUMNS).astype(BF16)
        for at in range(0, width, 128):
            fix = dot(all_ref[at : at + 128, g + 128 : g + 256], seen[...], MATMUL)
            model = all_ref[at : at + 128, 0:g].astype(F32) - fix
            all_ref[at : at + 128, 0:g] = model.astype(BF16)
        sources = [
            total(dot(stacked(obs_ref[k : k + 1, :], 16), all_ref[:, g + 128 : g + 256], BY_ROWS))
            for k in range(2)
        ]
        src_ref[0:1, :] = sources[0]
        src_ref[1:2, :] = sources[1]


def models(observations, held):
    vmem = pl.BlockSpec(memory_space=pltpu.VMEM)
    width, lanes = held.shape
    return pl.pallas_call(
        models_kernel,
        in_specs=[vmem] * 2,
        out_shape=(
            jax.ShapeDtypeStruct((width, lanes), BF16),
            jax.ShapeDtypeStruct((2, width), F32),
        ),
        scratch_shapes=[pltpu.VMEM((128, 2 * width), BF16)],
        input_output_aliases={1: 0},
        compiler_params=pltpu.CompilerParams(vmem_limit_bytes=16 << 20),
        cost_estimate=pl.CostEstimate(
            flops=512 * width**2, bytes_accessed=8 * width * width, transcendentals=0
        ),
        name="models",
    )(observations, held)


def product_kernel(all_ref, src_ref, after_ref, both_ref, sum_ref):
    del after_ref
    width = all_ref.shape[0]
    g = 2 * width

    @pl.when(lax.axis_index("tm") > 1)
    def _():
        sum_ref[...] = step(all_ref[:, width:g], src_ref[0:1, :], src_ref[1:2, :])
        for at in range(0, width, 256):
            rows = all_ref[at : at + 256, width:g]
            both_ref[at : at + 256, :] = dot(rows, all_ref[:, 0:width], MATMUL).astype(BF16)


def product(held, sources, after):
    width = held.shape[0]
    return pl.pallas_call(
        product_kernel,
        in_specs=[pl.BlockSpec(memory_space=pltpu.VMEM)] * 3,
        out_shape=(
            jax.ShapeDtypeStruct((width, width), BF16),
            jax.ShapeDtypeStruct((1, width), F32),
        ),
        compiler_params=pltpu.CompilerParams(vmem_limit_bytes=8 << 20),
        cost_estimate=pl.CostEstimate(
            flops=2 * width**3, bytes_accessed=6 * width * width, transcendentals=0
        ),
        name="product",
    )(held, sources, after)


def second_kernel(all_ref, src_ref, x_ref, end0, kept0, end_ref, kept_ref):
    mine = lax.axis_index("tm") == 1

    @pl.when(mine)
    def _():
        width = all_ref.shape[0]
        u = step(all_ref[:, 0:width], x_ref[...], src_ref[0:1, :])
        end_ref[...] = step(all_ref[:, width : 2 * width], u, src_ref[1:2, :])
        kept_ref[...] = u

    @pl.when(jnp.logical_not(mine))
    def _():
        end_ref[...] = end0[...]
        kept_ref[...] = kept0[...]


def second(held, sources, x, end, kept):
    row = jax.ShapeDtypeStruct(x.shape, F32)
    return pl.pallas_call(
        second_kernel,
        in_specs=[pl.BlockSpec(memory_space=pltpu.VMEM)] * 5,
        out_shape=(row, row),
        compiler_params=pltpu.CompilerParams(vmem_limit_bytes=4 << 20),
        name="second",
    )(held, sources, x, end, kept)


def advance_kernel(block, both_ref, sum_ref, x_ref, end0, kept0, end_ref, kept_ref):
    mine = lax.axis_index("tm") == block

    @pl.when(mine)
    def _():
        x = x_ref[...]
        end_ref[...] = step(both_ref[...], x, sum_ref[...])
        kept_ref[...] = x

    @pl.when(jnp.logical_not(mine))
    def _():
        end_ref[...] = end0[...]
        kept_ref[...] = kept0[...]


def advance(block, both, sums, x, end, kept):
    row = jax.ShapeDtypeStruct(x.shape, F32)
    return pl.pallas_call(
        functools.partial(advance_kernel, block),
        in_specs=[pl.BlockSpec(memory_space=pltpu.VMEM)] * 5,
        out_shape=(row, row),
        compiler_params=pltpu.CompilerParams(vmem_limit_bytes=4 << 20),
        name="advance",
    )(both, sums, x, end, kept)


def finish_kernel(all_ref, both_ref, src_ref, sum_ref, x_ref, end_ref, kept_ref, means_ref, last_ref, held):
    rows, width = means_ref.shape[1], all_ref.shape[0]
    here = lax.axis_index("tm")
    held[0:1, :] = kept_ref[...]
    held[1:2, :] = end_ref[...]

    @pl.when(here == BLOCKS - 1)
    def _():
        held[0:1, :] = step(all_ref[:, 0:width], x_ref[...], src_ref[0:1, :])
        held[1:2, :] = step(both_ref[...], x_ref[...], sum_ref[...])

    @pl.when(jnp.logical_and(here > 1, here < BLOCKS - 1))
    def _():
        held[0:1, :] = step(all_ref[:, 0:width], kept_ref[...], src_ref[0:1, :])

    mine = pltpu.roll(held[...], lanes_shift(rows, width), 1)
    means_ref[...] = mine[0:2, 0:rows]
    last_ref[...] = mine[1:2, 0:rows]


def finish(held, both, sources, sums, x, end, kept, rows):
    return pl.pallas_call(
        finish_kernel,
        in_specs=[pl.BlockSpec(memory_space=pltpu.VMEM)] * 7,
        out_shape=(
            jax.ShapeDtypeStruct((2, rows), F32),
            jax.ShapeDtypeStruct((1, rows), F32),
        ),
        scratch_shapes=[pltpu.VMEM((8, held.shape[0]), F32)],
        compiler_params=pltpu.CompilerParams(vmem_limit_bytes=4 << 20),
        name="finish",
    )(held, both, sources, sums, x, end, kept)


def along(first, distance):
    route = []
    for index in range(2 * RING * RING):
        z, y, core = place(index)
        if (core == 0) == first:
            route.append((index, index_of(z, y + distance, core)))
        else:
            route.append((index, index_of(z + distance, y, core)))
    return route


SWAP = [(index, index ^ 1) for index in range(2 * RING * RING)]


def shards(transitions, gain, obs_op, observations, start):
    rows, width = transitions.shape[1], transitions.shape[2]
    mine = pack(transitions, gain, obs_op, start)
    near = [mine] + [lax.ppermute(mine, "state", along(True, d)) for d in NEAR[1:]]
    line = jnp.concatenate(near, axis=0)
    ahead = lax.ppermute(line, "state", along(False, 1))
    behind = lax.ppermute(line, "state", along(False, RING - 1))
    half = line.shape[0] // 2
    across = [
        lax.ppermute(ahead[:half], "state", along(False, 1)),
        lax.ppermute(behind[half:], "state", along(False, RING - 1)),
    ]
    across = jnp.concatenate(across, axis=0)
    near_parts = [line, ahead, behind]
    near_parts += [lax.ppermute(part, "state", SWAP) for part in near_parts]
    held = early(near_parts, width)
    across = (across, lax.ppermute(across, "state", SWAP))
    held, end, kept = late(observations, across, held)
    x = lax.ppermute(end, "tm", [(0, 1)])
    held, sources = models(observations, held)
    end, kept = second(held, sources, x, end, kept)
    both, sums = product(held, sources, end)
    for block in range(2, BLOCKS - 1):
        x = lax.ppermute(end, "tm", [(block - 1, block)])
        end, kept = advance(block, both, sums, x, end, kept)
    x = lax.ppermute(end, "tm", [(BLOCKS - 2, BLOCKS - 1)])
    return finish(held, both, sources, sums, x, end, kept, rows)


def solution(mesh):
    in_specs = (
        P("tm", "state", None),
        P("state", None),
        P(None, "state"),
        P("tm", None),
        P("state"),
    )
    out_specs = (P("tm", "state"), P("tm", "state"))
    return jax.shard_map(shards, mesh=mesh, in_specs=in_specs, out_specs=out_specs, check_vma=False)
```

```python
import functools

import jax
import jax.numpy as jnp
from jax import lax
from jax.experimental import pallas as pl
from jax.experimental.pallas import tpu as pltpu
from jax.sharding import PartitionSpec as P

F32 = jnp.float32
BF16 = jnp.bfloat16
RING = 4
BLOCKS = 4
MATMUL = (((1,), (0,)), ((), ()))
BY_ROWS = (((1,), (1,)), ((), ()))
BY_COLUMNS = (((0,), (0,)), ((), ()))


def dot(left, right, dims):
    return lax.dot_general(left, right, dims, preferred_element_type=F32)


def split(x):
    high = x.astype(BF16)
    rest = x - high.astype(F32)
    mid = rest.astype(BF16)
    low = (rest - mid.astype(F32)).astype(BF16)
    return high, mid, low


def stacked(x, rows):
    pieces = jnp.concatenate([piece.astype(F32) for piece in split(x)], axis=0)
    pad = jnp.zeros((rows - pieces.shape[0], x.shape[1]), F32)
    return jnp.concatenate([pieces, pad], axis=0).astype(BF16)


def step(model, x, source):
    parts = dot(stacked(x, 16), model, BY_ROWS)
    return parts[0:1] + parts[1:2] + parts[2:3] + source


def pack_kernel(trans_ref, gain_ref, obs_ref, start_ref, out_ref, held, sems):
    rows, width = trans_ref.shape[1], trans_ref.shape[2]
    g = 2 * width
    copies = [
        pltpu.make_async_copy(start_ref, held, sems.at[0]),
        pltpu.make_async_copy(trans_ref.at[0], out_ref.at[:, 0:width], sems.at[1]),
        pltpu.make_async_copy(trans_ref.at[1], out_ref.at[:, width:g], sems.at[2]),
        pltpu.make_async_copy(obs_ref, out_ref.at[:, g : g + 128], sems.at[3]),
        pltpu.make_async_copy(gain_ref, out_ref.at[:, g + 128 : g + 256], sems.at[4]),
    ]
    for copy in copies:
        copy.start()
    eye = (
        lax.broadcasted_iota(jnp.int32, (rows, rows), 0)
        == lax.broadcasted_iota(jnp.int32, (rows, rows), 1)
    ).astype(F32).astype(BF16)
    copies[0].wait()
    out_ref[:, g + 256 :] = dot(eye, stacked(held[...], 128), BY_ROWS).astype(BF16)
    for copy in copies[1:]:
        copy.wait()


def pack(transitions, gain, obs_op, start):
    rows, width = transitions.shape[1], transitions.shape[2]
    return pl.pallas_call(
        pack_kernel,
        in_specs=[pl.BlockSpec(memory_space=pltpu.HBM)] * 4,
        out_shape=jax.ShapeDtypeStruct((rows, 2 * width + 384), BF16),
        scratch_shapes=[pltpu.VMEM((1, rows), F32), pltpu.SemaphoreType.DMA((5,))],
        compiler_params=pltpu.CompilerParams(vmem_limit_bytes=4 << 20),
        name="pack",
    )(*(pltpu.with_memory_space_constraint(x, pltpu.HBM) for x in (transitions, gain, obs_op.T, start[None, :])))


def place(index):
    return index // (2 * RING), (index // 2) % RING, index % 2


def index_of(z, y, core):
    return ((z % RING) * RING + y % RING) * 2 + core


NEAR = (0, 3, 2, 1)
EARLY, LATE = (0, 1, RING - 1), (2,)


def row_offsets(rows, fars):
    z, y, core = place(lax.axis_index("state"))
    z, y = z + RING, y + RING
    offsets = []
    for side in (core, 1 - core):
        for far in fars:
            for near in NEAR:
                dz = far + side * (near - far)
                dy = near + side * (far - near)
                offsets.append(rows * index_of(z - dz, y - dy, side))
    return offsets


def put_rows(parts, fars, out_ref):
    rows = parts[0].shape[0] // RING
    where = row_offsets(rows, fars)
    for index, part in enumerate(parts):
        for j in range(RING):
            at = pl.multiple_of(where[index * RING + j], rows)
            out_ref[pl.ds(at, rows), :] = part[j * rows : (j + 1) * rows, :]


def early_kernel(*refs):
    put_rows(refs[:-1], EARLY, refs[-1])


def early(parts, width):
    vmem = pl.BlockSpec(memory_space=pltpu.VMEM)
    return pl.pallas_call(
        early_kernel,
        in_specs=[vmem] * len(parts),
        out_shape=jax.ShapeDtypeStruct((width, parts[0].shape[1]), BF16),
        compiler_params=pltpu.CompilerParams(vmem_limit_bytes=4 << 20),
        name="early",
    )(*parts)


def total(parts):
    return parts[0:1] + parts[1:2] + parts[2:3]


def late_kernel(
    obs_ref, part0, part1, held_ref, all_ref, end_ref, kept_ref
):
    del held_ref
    width = all_ref.shape[0]
    g = 2 * width
    put_rows((part0, part1), LATE, all_ref)
    is_first = lax.axis_index("tm") == 0

    @pl.when(is_first)
    def _():
        pick = (
            lax.broadcasted_iota(jnp.int32, (16, 128), 0)
            == lax.broadcasted_iota(jnp.int32, (16, 128), 1)
        ).astype(F32).astype(BF16)
        x = total(dot(pick, all_ref[:, g + 256 : g + 384], BY_ROWS))
        states = []
        for k in range(2):
            y = total(dot(stacked(x, 16), all_ref[:, k * width : (k + 1) * width], BY_ROWS))
            seen_y = total(dot(stacked(y, 16), all_ref[:, g : g + 128], MATMUL))
            missed = stacked(obs_ref[k : k + 1, :] - seen_y, 16)
            x = y + total(dot(missed, all_ref[:, g + 128 : g + 256], BY_ROWS))
            states.append(x)
        kept_ref[...] = states[0]
        end_ref[...] = states[1]

    @pl.when(jnp.logical_not(is_first))
    def _():
        kept_ref[...] = jnp.zeros_like(kept_ref)
        end_ref[...] = jnp.zeros_like(end_ref)


def late(observations, parts, held):
    vmem = pl.BlockSpec(memory_space=pltpu.VMEM)
    width, lanes = held.shape
    row = jax.ShapeDtypeStruct((1, width), F32)
    return pl.pallas_call(
        late_kernel,
        in_specs=[vmem] * 4,
        out_shape=(jax.ShapeDtypeStruct((width, lanes), BF16), row, row),
        input_output_aliases={3: 0},
        compiler_params=pltpu.CompilerParams(vmem_limit_bytes=4 << 20),
        name="late",
    )(observations, *parts, held)


def models_kernel(obs_ref, held_ref, all_ref, src_ref, seen):
    del held_ref
    width = all_ref.shape[0]
    g = 2 * width

    @pl.when(lax.axis_index("tm") > 0)
    def _():
        seen[...] = dot(all_ref[:, g : g + 128], all_ref[:, 0:g], BY_COLUMNS).astype(BF16)
        for at in range(0, width, 128):
            fix = dot(all_ref[at : at + 128, g + 128 : g + 256], seen[...], MATMUL)
            model = all_ref[at : at + 128, 0:g].astype(F32) - fix
            all_ref[at : at + 128, 0:g] = model.astype(BF16)
        sources = [
            total(dot(stacked(obs_ref[k : k + 1, :], 16), all_ref[:, g + 128 : g + 256], BY_ROWS))
            for k in range(2)
        ]
        src_ref[0:1, :] = sources[0]
        src_ref[1:2, :] = sources[1]


def models(observations, held):
    vmem = pl.BlockSpec(memory_space=pltpu.VMEM)
    width, lanes = held.shape
    return pl.pallas_call(
        models_kernel,
        in_specs=[vmem] * 2,
        out_shape=(
            jax.ShapeDtypeStruct((width, lanes), BF16),
            jax.ShapeDtypeStruct((2, width), F32),
        ),
        scratch_shapes=[pltpu.VMEM((128, 2 * width), BF16)],
        input_output_aliases={1: 0},
        compiler_params=pltpu.CompilerParams(vmem_limit_bytes=16 << 20),
        cost_estimate=pl.CostEstimate(
            flops=512 * width**2, bytes_accessed=8 * width * width, transcendentals=0
        ),
        name="models",
    )(observations, held)


def product_kernel(all_ref, src_ref, after_ref, both_ref, sum_ref):
    del after_ref
    width = all_ref.shape[0]
    g = 2 * width

    @pl.when(lax.axis_index("tm") > 1)
    def _():
        sum_ref[...] = step(all_ref[:, width:g], src_ref[0:1, :], src_ref[1:2, :])
        for at in range(0, width, 256):
            rows = all_ref[at : at + 256, width:g]
            both_ref[at : at + 256, :] = dot(rows, all_ref[:, 0:width], MATMUL).astype(BF16)


def product(held, sources, after):
    width = held.shape[0]
    return pl.pallas_call(
        product_kernel,
        in_specs=[pl.BlockSpec(memory_space=pltpu.VMEM)] * 3,
        out_shape=(
            jax.ShapeDtypeStruct((width, width), BF16),
            jax.ShapeDtypeStruct((1, width), F32),
        ),
        compiler_params=pltpu.CompilerParams(vmem_limit_bytes=8 << 20),
        cost_estimate=pl.CostEstimate(
            flops=2 * width**3, bytes_accessed=6 * width * width, transcendentals=0
        ),
        name="product",
    )(held, sources, after)


def second_kernel(all_ref, src_ref, x_ref, end0, kept0, end_ref, kept_ref):
    mine = lax.axis_index("tm") == 1

    @pl.when(mine)
    def _():
        width = all_ref.shape[0]
        u = step(all_ref[:, 0:width], x_ref[...], src_ref[0:1, :])
        end_ref[...] = step(all_ref[:, width : 2 * width], u, src_ref[1:2, :])
        kept_ref[...] = u

    @pl.when(jnp.logical_not(mine))
    def _():
        end_ref[...] = end0[...]
        kept_ref[...] = kept0[...]


def second(held, sources, x, end, kept):
    row = jax.ShapeDtypeStruct(x.shape, F32)
    return pl.pallas_call(
        second_kernel,
        in_specs=[pl.BlockSpec(memory_space=pltpu.VMEM)] * 5,
        out_shape=(row, row),
        compiler_params=pltpu.CompilerParams(vmem_limit_bytes=4 << 20),
        name="second",
    )(held, sources, x, end, kept)


def advance_kernel(block, both_ref, sum_ref, x_ref, end0, kept0, end_ref, kept_ref):
    mine = lax.axis_index("tm") == block

    @pl.when(mine)
    def _():
        x = x_ref[...]
        end_ref[...] = step(both_ref[...], x, sum_ref[...])
        kept_ref[...] = x

    @pl.when(jnp.logical_not(mine))
    def _():
        end_ref[...] = end0[...]
        kept_ref[...] = kept0[...]


def advance(block, both, sums, x, end, kept):
    row = jax.ShapeDtypeStruct(x.shape, F32)
    return pl.pallas_call(
        functools.partial(advance_kernel, block),
        in_specs=[pl.BlockSpec(memory_space=pltpu.VMEM)] * 5,
        out_shape=(row, row),
        compiler_params=pltpu.CompilerParams(vmem_limit_bytes=4 << 20),
        name="advance",
    )(both, sums, x, end, kept)


def finish_kernel(all_ref, both_ref, src_ref, sum_ref, x_ref, end_ref, kept_ref, means_ref, last_ref, held):
    rows, width = means_ref.shape[1], all_ref.shape[0]
    here = lax.axis_index("tm")
    held[0:1, :] = kept_ref[...]
    held[1:2, :] = end_ref[...]

    @pl.when(here == BLOCKS - 1)
    def _():
        held[0:1, :] = step(all_ref[:, 0:width], x_ref[...], src_ref[0:1, :])
        held[1:2, :] = step(both_ref[...], x_ref[...], sum_ref[...])

    @pl.when(jnp.logical_and(here > 1, here < BLOCKS - 1))
    def _():
        held[0:1, :] = step(all_ref[:, 0:width], kept_ref[...], src_ref[0:1, :])

    offset = rows * lax.axis_index("state")
    inside = lax.rem(offset, 128)
    lanes = held[:, pl.ds(pl.multiple_of(offset - inside, 128), 128)]
    mine = pltpu.roll(lanes, lax.rem(128 - inside, 128), 1)
    means_ref[...] = mine[0:2, 0:rows]
    last_ref[...] = mine[1:2, 0:rows]


def finish(held, both, sources, sums, x, end, kept, rows):
    return pl.pallas_call(
        finish_kernel,
        in_specs=[pl.BlockSpec(memory_space=pltpu.VMEM)] * 7,
        out_shape=(
            jax.ShapeDtypeStruct((2, rows), F32),
            jax.ShapeDtypeStruct((1, rows), F32),
        ),
        scratch_shapes=[pltpu.VMEM((8, held.shape[0]), F32)],
        compiler_params=pltpu.CompilerParams(vmem_limit_bytes=4 << 20),
        name="finish",
    )(held, both, sources, sums, x, end, kept)


def along(first, distance):
    route = []
    for index in range(2 * RING * RING):
        z, y, core = place(index)
        if (core == 0) == first:
            route.append((index, index_of(z, y + distance, core)))
        else:
            route.append((index, index_of(z + distance, y, core)))
    return route


SWAP = [(index, index ^ 1) for index in range(2 * RING * RING)]


def shards(transitions, gain, obs_op, observations, start):
    rows, width = transitions.shape[1], transitions.shape[2]
    mine = pack(transitions, gain, obs_op, start)
    near = [mine] + [lax.ppermute(mine, "state", along(True, d)) for d in NEAR[1:]]
    line = jnp.concatenate(near, axis=0)
    ahead = lax.ppermute(line, "state", along(False, 1))
    behind = lax.ppermute(line, "state", along(False, RING - 1))
    half = line.shape[0] // 2
    across = [
        lax.ppermute(ahead[:half], "state", along(False, 1)),
        lax.ppermute(behind[half:], "state", along(False, RING - 1)),
    ]
    across = jnp.concatenate(across, axis=0)
    near_parts = [line, ahead, behind]
    near_parts += [lax.ppermute(part, "state", SWAP) for part in near_parts]
    held = early(near_parts, width)
    across = (across, lax.ppermute(across, "state", SWAP))
    held, end, kept = late(observations, across, held)
    x = lax.ppermute(end, "tm", [(0, 1)])
    held, sources = models(observations, held)
    end, kept = second(held, sources, x, end, kept)
    both, sums = product(held, sources, end)
    for block in range(2, BLOCKS - 1):
        x = lax.ppermute(end, "tm", [(block - 1, block)])
        end, kept = advance(block, both, sums, x, end, kept)
    x = lax.ppermute(end, "tm", [(BLOCKS - 2, BLOCKS - 1)])
    return finish(held, both, sources, sums, x, end, kept, rows)


def solution(mesh):
    in_specs = (
        P("tm", "state", None),
        P("state", None),
        P(None, "state"),
        P("tm", None),
        P("state"),
    )
    out_specs = (P("tm", "state"), P("tm", "state"))
    return jax.shard_map(shards, mesh=mesh, in_specs=in_specs, out_specs=out_specs, check_vma=False)
```

```python
import functools

import jax
import jax.numpy as jnp
from jax import lax
from jax.experimental import pallas as pl
from jax.experimental.pallas import tpu as pltpu
from jax.sharding import PartitionSpec as P

F32 = jnp.float32
BF16 = jnp.bfloat16
RING = 4
BLOCKS = 4
MATMUL = (((1,), (0,)), ((), ()))
BY_ROWS = (((1,), (1,)), ((), ()))
BY_COLUMNS = (((0,), (0,)), ((), ()))


def dot(left, right, dims):
    return lax.dot_general(left, right, dims, preferred_element_type=F32)


def split(x):
    high = x.astype(BF16)
    rest = x - high.astype(F32)
    mid = rest.astype(BF16)
    low = (rest - mid.astype(F32)).astype(BF16)
    return high, mid, low


def stacked(x, rows):
    pieces = jnp.concatenate([piece.astype(F32) for piece in split(x)], axis=0)
    pad = jnp.zeros((rows - pieces.shape[0], x.shape[1]), F32)
    return jnp.concatenate([pieces, pad], axis=0).astype(BF16)


def step(model, x, source):
    parts = dot(stacked(x, 16), model, BY_ROWS)
    return parts[0:1] + parts[1:2] + parts[2:3] + source


def pack_kernel(trans_ref, gain_ref, obs_ref, start_ref, out_ref, held, sems):
    rows, width = trans_ref.shape[1], trans_ref.shape[2]
    g = 2 * width
    copies = [
        pltpu.make_async_copy(start_ref, held, sems.at[0]),
        pltpu.make_async_copy(trans_ref.at[0], out_ref.at[:, 0:width], sems.at[1]),
        pltpu.make_async_copy(trans_ref.at[1], out_ref.at[:, width:g], sems.at[2]),
        pltpu.make_async_copy(obs_ref, out_ref.at[:, g : g + 128], sems.at[3]),
        pltpu.make_async_copy(gain_ref, out_ref.at[:, g + 128 : g + 256], sems.at[4]),
    ]
    for copy in copies:
        copy.start()
    eye = (
        lax.broadcasted_iota(jnp.int32, (rows, rows), 0)
        == lax.broadcasted_iota(jnp.int32, (rows, rows), 1)
    ).astype(F32).astype(BF16)
    copies[0].wait()
    out_ref[:, g + 256 :] = dot(eye, stacked(held[...], 128), BY_ROWS).astype(BF16)
    for copy in copies[1:]:
        copy.wait()


def pack(transitions, gain, obs_op, start):
    rows, width = transitions.shape[1], transitions.shape[2]
    return pl.pallas_call(
        pack_kernel,
        in_specs=[pl.BlockSpec(memory_space=pltpu.HBM)] * 4,
        out_shape=jax.ShapeDtypeStruct((rows, 2 * width + 384), BF16),
        scratch_shapes=[pltpu.VMEM((1, rows), F32), pltpu.SemaphoreType.DMA((5,))],
        compiler_params=pltpu.CompilerParams(vmem_limit_bytes=4 << 20),
        name="pack",
    )(*(pltpu.with_memory_space_constraint(x, pltpu.HBM) for x in (transitions, gain, obs_op.T, start[None, :])))


def place(index):
    return index // (2 * RING), (index // 2) % RING, index % 2


def index_of(z, y, core):
    return ((z % RING) * RING + y % RING) * 2 + core


NEAR = (3, 0, 2, 1)
EARLY, LATE = (0, 1, RING - 1), (2,)


def row_offsets(rows, fars):
    z, y, core = place(lax.axis_index("state"))
    z, y = z + RING, y + RING
    offsets = []
    for side in (core, 1 - core):
        for far in fars:
            for near in NEAR:
                dz = far + side * (near - far)
                dy = near + side * (far - near)
                offsets.append(rows * index_of(z - dz, y - dy, side))
    return offsets


def put_rows(parts, fars, out_ref):
    rows = parts[0].shape[0] // RING
    where = row_offsets(rows, fars)
    for index, part in enumerate(parts):
        for j in range(RING):
            at = pl.multiple_of(where[index * RING + j], rows)
            out_ref[pl.ds(at, rows), :] = part[j * rows : (j + 1) * rows, :]


def lanes_shift(rows, width):
    return lax.rem(width - rows * lax.axis_index("state"), width)


def early_kernel(*refs):
    put_rows(refs[:-1], EARLY, refs[-1])


def early(parts, width):
    vmem = pl.BlockSpec(memory_space=pltpu.VMEM)
    return pl.pallas_call(
        early_kernel,
        in_specs=[vmem] * len(parts),
        out_shape=jax.ShapeDtypeStruct((width, parts[0].shape[1]), BF16),
        compiler_params=pltpu.CompilerParams(vmem_limit_bytes=4 << 20),
        name="early",
    )(*parts)


def total(parts):
    return parts[0:1] + parts[1:2] + parts[2:3]


def late_kernel(
    obs_ref, part0, part1, held_ref, all_ref, end_ref, kept_ref
):
    del held_ref
    width = all_ref.shape[0]
    g = 2 * width
    put_rows((part0, part1), LATE, all_ref)
    is_first = lax.axis_index("tm") == 0

    @pl.when(is_first)
    def _():
        pick = (
            lax.broadcasted_iota(jnp.int32, (16, 128), 0)
            == lax.broadcasted_iota(jnp.int32, (16, 128), 1)
        ).astype(F32).astype(BF16)
        x = total(dot(pick, all_ref[:, g + 256 : g + 384], BY_ROWS))
        states = []
        for k in range(2):
            y = total(dot(stacked(x, 16), all_ref[:, k * width : (k + 1) * width], BY_ROWS))
            seen_y = total(dot(stacked(y, 16), all_ref[:, g : g + 128], MATMUL))
            missed = stacked(obs_ref[k : k + 1, :] - seen_y, 16)
            x = y + total(dot(missed, all_ref[:, g + 128 : g + 256], BY_ROWS))
            states.append(x)
        kept_ref[...] = states[0]
        end_ref[...] = states[1]

    @pl.when(jnp.logical_not(is_first))
    def _():
        kept_ref[...] = jnp.zeros_like(kept_ref)
        end_ref[...] = jnp.zeros_like(end_ref)


def late(observations, parts, held):
    vmem = pl.BlockSpec(memory_space=pltpu.VMEM)
    width, lanes = held.shape
    row = jax.ShapeDtypeStruct((1, width), F32)
    return pl.pallas_call(
        late_kernel,
        in_specs=[vmem] * 4,
        out_shape=(jax.ShapeDtypeStruct((width, lanes), BF16), row, row),
        input_output_aliases={3: 0},
        compiler_params=pltpu.CompilerParams(vmem_limit_bytes=4 << 20),
        name="late",
    )(observations, *parts, held)


def models_kernel(obs_ref, held_ref, all_ref, src_ref, seen):
    del held_ref
    width = all_ref.shape[0]
    g = 2 * width

    @pl.when(lax.axis_index("tm") > 0)
    def _():
        seen[...] = dot(all_ref[:, g : g + 128], all_ref[:, 0:g], BY_COLUMNS).astype(BF16)
        for at in range(0, width, 128):
            fix = dot(all_ref[at : at + 128, g + 128 : g + 256], seen[...], MATMUL)
            model = all_ref[at : at + 128, 0:g].astype(F32) - fix
            all_ref[at : at + 128, 0:g] = model.astype(BF16)
        sources = [
            total(dot(stacked(obs_ref[k : k + 1, :], 16), all_ref[:, g + 128 : g + 256], BY_ROWS))
            for k in range(2)
        ]
        src_ref[0:1, :] = sources[0]
        src_ref[1:2, :] = sources[1]


def models(observations, held):
    vmem = pl.BlockSpec(memory_space=pltpu.VMEM)
    width, lanes = held.shape
    return pl.pallas_call(
        models_kernel,
        in_specs=[vmem] * 2,
        out_shape=(
            jax.ShapeDtypeStruct((width, lanes), BF16),
            jax.ShapeDtypeStruct((2, width), F32),
        ),
        scratch_shapes=[pltpu.VMEM((128, 2 * width), BF16)],
        input_output_aliases={1: 0},
        compiler_params=pltpu.CompilerParams(vmem_limit_bytes=16 << 20),
        cost_estimate=pl.CostEstimate(
            flops=512 * width**2, bytes_accessed=8 * width * width, transcendentals=0
        ),
        name="models",
    )(observations, held)


def product_kernel(all_ref, src_ref, after_ref, both_ref, sum_ref):
    del after_ref
    width = all_ref.shape[0]
    g = 2 * width

    @pl.when(lax.axis_index("tm") > 1)
    def _():
        sum_ref[...] = step(all_ref[:, width:g], src_ref[0:1, :], src_ref[1:2, :])
        for at in range(0, width, 256):
            rows = all_ref[at : at + 256, width:g]
            both_ref[at : at + 256, :] = dot(rows, all_ref[:, 0:width], MATMUL).astype(BF16)


def product(held, sources, after):
    width = held.shape[0]
    return pl.pallas_call(
        product_kernel,
        in_specs=[pl.BlockSpec(memory_space=pltpu.VMEM)] * 3,
        out_shape=(
            jax.ShapeDtypeStruct((width, width), BF16),
            jax.ShapeDtypeStruct((1, width), F32),
        ),
        compiler_params=pltpu.CompilerParams(vmem_limit_bytes=8 << 20),
        cost_estimate=pl.CostEstimate(
            flops=2 * width**3, bytes_accessed=6 * width * width, transcendentals=0
        ),
        name="product",
    )(held, sources, after)


def second_kernel(all_ref, src_ref, x_ref, end0, kept0, end_ref, kept_ref):
    mine = lax.axis_index("tm") == 1

    @pl.when(mine)
    def _():
        width = all_ref.shape[0]
        u = step(all_ref[:, 0:width], x_ref[...], src_ref[0:1, :])
        end_ref[...] = step(all_ref[:, width : 2 * width], u, src_ref[1:2, :])
        kept_ref[...] = u

    @pl.when(jnp.logical_not(mine))
    def _():
        end_ref[...] = end0[...]
        kept_ref[...] = kept0[...]


def second(held, sources, x, end, kept):
    row = jax.ShapeDtypeStruct(x.shape, F32)
    return pl.pallas_call(
        second_kernel,
        in_specs=[pl.BlockSpec(memory_space=pltpu.VMEM)] * 5,
        out_shape=(row, row),
        compiler_params=pltpu.CompilerParams(vmem_limit_bytes=4 << 20),
        name="second",
    )(held, sources, x, end, kept)


def advance_kernel(block, both_ref, sum_ref, x_ref, end0, kept0, end_ref, kept_ref):
    mine = lax.axis_index("tm") == block

    @pl.when(mine)
    def _():
        x = x_ref[...]
        end_ref[...] = step(both_ref[...], x, sum_ref[...])
        kept_ref[...] = x

    @pl.when(jnp.logical_not(mine))
    def _():
        end_ref[...] = end0[...]
        kept_ref[...] = kept0[...]


def advance(block, both, sums, x, end, kept):
    row = jax.ShapeDtypeStruct(x.shape, F32)
    return pl.pallas_call(
        functools.partial(advance_kernel, block),
        in_specs=[pl.BlockSpec(memory_space=pltpu.VMEM)] * 5,
        out_shape=(row, row),
        compiler_params=pltpu.CompilerParams(vmem_limit_bytes=4 << 20),
        name="advance",
    )(both, sums, x, end, kept)


def finish_kernel(all_ref, both_ref, src_ref, sum_ref, x_ref, end_ref, kept_ref, means_ref, last_ref, held):
    rows, width = means_ref.shape[1], all_ref.shape[0]
    here = lax.axis_index("tm")
    held[0:1, :] = kept_ref[...]
    held[1:2, :] = end_ref[...]

    @pl.when(here == BLOCKS - 1)
    def _():
        held[0:1, :] = step(all_ref[:, 0:width], x_ref[...], src_ref[0:1, :])
        held[1:2, :] = step(both_ref[...], x_ref[...], sum_ref[...])

    @pl.when(jnp.logical_and(here > 1, here < BLOCKS - 1))
    def _():
        held[0:1, :] = step(all_ref[:, 0:width], kept_ref[...], src_ref[0:1, :])

    mine = pltpu.roll(held[...], lanes_shift(rows, width), 1)
    means_ref[...] = mine[0:2, 0:rows]
    last_ref[...] = mine[1:2, 0:rows]


def finish(held, both, sources, sums, x, end, kept, rows):
    return pl.pallas_call(
        finish_kernel,
        in_specs=[pl.BlockSpec(memory_space=pltpu.VMEM)] * 7,
        out_shape=(
            jax.ShapeDtypeStruct((2, rows), F32),
            jax.ShapeDtypeStruct((1, rows), F32),
        ),
        scratch_shapes=[pltpu.VMEM((8, held.shape[0]), F32)],
        compiler_params=pltpu.CompilerParams(vmem_limit_bytes=4 << 20),
        name="finish",
    )(held, both, sources, sums, x, end, kept)


def along(first, distance):
    route = []
    for index in range(2 * RING * RING):
        z, y, core = place(index)
        if (core == 0) == first:
            route.append((index, index_of(z, y + distance, core)))
        else:
            route.append((index, index_of(z + distance, y, core)))
    return route


SWAP = [(index, index ^ 1) for index in range(2 * RING * RING)]


def shards(transitions, gain, obs_op, observations, start):
    rows, width = transitions.shape[1], transitions.shape[2]
    mine = pack(transitions, gain, obs_op, start)
    near = [mine if d == 0 else lax.ppermute(mine, "state", along(True, d)) for d in NEAR]
    line = jnp.concatenate(near, axis=0)
    ahead = lax.ppermute(line, "state", along(False, 1))
    behind = lax.ppermute(line, "state", along(False, RING - 1))
    half = line.shape[0] // 2
    across = [
        lax.ppermute(ahead[:half], "state", along(False, 1)),
        lax.ppermute(behind[half:], "state", along(False, RING - 1)),
    ]
    across = jnp.concatenate(across, axis=0)
    near_parts = [line, ahead, behind]
    near_parts += [lax.ppermute(part, "state", SWAP) for part in near_parts]
    held = early(near_parts, width)
    across = (across, lax.ppermute(across, "state", SWAP))
    held, end, kept = late(observations, across, held)
    x = lax.ppermute(end, "tm", [(0, 1)])
    held, sources = models(observations, held)
    end, kept = second(held, sources, x, end, kept)
    both, sums = product(held, sources, end)
    for block in range(2, BLOCKS - 1):
        x = lax.ppermute(end, "tm", [(block - 1, block)])
        end, kept = advance(block, both, sums, x, end, kept)
    x = lax.ppermute(end, "tm", [(BLOCKS - 2, BLOCKS - 1)])
    return finish(held, both, sources, sums, x, end, kept, rows)


def solution(mesh):
    in_specs = (
        P("tm", "state", None),
        P("state", None),
        P(None, "state"),
        P("tm", None),
        P("state"),
    )
    out_specs = (P("tm", "state"), P("tm", "state"))
    return jax.shard_map(shards, mesh=mesh, in_specs=in_specs, out_specs=out_specs, check_vma=False)
```
